512 devices in a mesh: frame: 64 (over z, x), head: 8 (over y, core).
Axes of the slice: x: 4, y: 4, z: 16, core: 2. Of those that a mesh axis runs over, the one named last changes fastest.
Arguments:
- queries: bfloat16 [24576, 3072], P(('frame', 'head')), as said below
- key_vectors: bfloat16 [24576, 3072], P(('frame', 'head')), as said below
- value_vectors: bfloat16 [24576, 3072], P(('frame', 'head')), may hold values from -6 to 6
- windows: int32 [64, 27], P('frame'), may hold values from 0 to 63, as said below
- counts: int32 [64], P('frame'), may hold values from 1 to 27, as said below
Outputs:
- attended: bfloat16 [24576, 3072], P(('frame', 'head'))
The draws below stay inside these ranges and needn't reach their ends.
Inputs may be any that keep to these rules, and one draw needn't show every extreme that they name: `windows`: tiles are numbered by layer, then row, then column in a grid of 4 x 4 x 4 tiles. Row t names tiles whose layer, row and column each differ from those of tile t by at most one; its first counts[t] entries are distinct and include t; the other entries equal t. `counts`: the number of live entries of each row of windows; some tile reaches 27 in every draw. `queries`: float entries; may be large in some rows. `key_vectors`: float entries.
All inputs are finite; a program needn't handle non-finite values.
Results may differ from the reference program's by a relative error of at most 0.012.
Values may be sent and summed in bfloat16 or wider, within the bound.
A program may use at most 128 MiB of HBM per device.

```python
import jax
import jax.numpy as jnp
from jax import lax

HEADS = 24
HEAD_DIM = 128
D = 3072
TILE = 384
HT = 4
WT = 4
WIN = 27
TILES = 64
TOKENS = 24576


def draw_queries(key, part):
    key = jax.random.fold_in(key, 1)
    bulk = jax.random.normal(key, (TOKENS, D), jnp.float32) * 1.5
    return bulk.astype(jnp.bfloat16)


def draw_key_vectors(key, part):
    key = jax.random.fold_in(key, 2)
    bulk = jax.random.normal(key, (TOKENS, D), jnp.float32) * 1.5
    return bulk.astype(jnp.bfloat16)


def window_lists(key):
    layer_size = HT * WT
    layers = TILES // layer_size
    tiles = jnp.arange(TILES, dtype=jnp.int32)
    layer = tiles // layer_size
    within = tiles % layer_size
    row_of = within // WT
    column = within % WT
    offsets = jnp.arange(27, dtype=jnp.int32)
    near_layer = layer[:, None] + offsets[None, :] // 9 - 1
    near_row = row_of[:, None] + offsets[None, :] // 3 % 3 - 1
    near_column = column[:, None] + offsets[None, :] % 3 - 1
    inside = (near_layer >= 0) & (near_layer < layers) & (near_row >= 0) & (near_row < HT) & (near_column >= 0) & (near_column < WT)
    drawn = jax.random.randint(jax.random.fold_in(key, 201), (TILES, 27), 0, 10) < 6
    centre = (offsets == 13)[None, :]
    forced = ((layer == min(1, layers - 1)) & (row_of == 1) & (column == 1))[:, None]
    keep = inside & (drawn | centre | forced)
    neighbour = (near_layer * HT + near_row) * WT + near_column
    order = jnp.argsort(jnp.where(keep, 0, 1).astype(jnp.int32), axis=1, stable=True)
    sorted_keep = jnp.take_along_axis(keep, order, axis=1)[:, :WIN]
    sorted_tiles = jnp.take_along_axis(neighbour, order, axis=1)[:, :WIN]
    lists = jnp.where(sorted_keep, sorted_tiles, tiles[:, None]).astype(jnp.int32)
    totals = jnp.sum(keep.astype(jnp.int32), axis=1).astype(jnp.int32)
    return (lists, totals)


def draw_windows(key, part):
    lists, totals = window_lists(key)
    return lists


def draw_counts(key, part):
    lists, totals = window_lists(key)
    return totals


def levels(key, dims, split, low, top_value):
    def one(dim, parts):
        draws = jax.random.uniform(jax.random.fold_in(jax.random.fold_in(key, 6), dim), (parts,), jnp.float32, low / len(split), top_value / len(split))
        return jnp.repeat(jnp.exp(draws), dims[dim] // parts).reshape((-1,) + (1,) * (len(dims) - dim - 1))

    loudness = one(*split[0])
    for cut in split[1:]:
        loudness = loudness * one(*cut)
    return loudness


def gaussian(rng, extent, width, reach, cuts=(), held_as=jnp.bfloat16):
    entries = jax.random.normal(rng, extent, jnp.float32) * width
    if len(cuts) > 0:
        entries = levels(rng, extent, cuts, -0.22, 0.18) * entries
    return jnp.clip(entries, min=-reach, max=reach).astype(held_as)


def setup_inputs(seed: int = 0) -> dict:
    seeds = jax.random.split(jax.random.key(seed), 6)
    return {
        "queries": draw_queries(jax.random.fold_in(seeds[5], 71), 0),
        "key_vectors": draw_key_vectors(jax.random.fold_in(seeds[5], 71), 0),
        "value_vectors": gaussian(seeds[2], (TOKENS, D), 1.0, 6.0, ((0, 512),)),
        "windows": draw_windows(jax.random.fold_in(seeds[5], 71), 0),
        "counts": draw_counts(jax.random.fold_in(seeds[5], 71), 0),
    }


def reference(queries, key_vectors, value_vectors, windows, counts):
    query_tiles = queries.reshape(TILES, TILE, HEADS, HEAD_DIM)
    key_tiles = key_vectors.reshape(TILES, TILE, HEADS, HEAD_DIM)
    value_tiles = value_vectors.reshape(TILES, TILE, HEADS, HEAD_DIM)
    inv_root = HEAD_DIM ** -0.5

    def one_tile(operands):
        tile_query, tile_list, tile_count = operands
        key_window = key_tiles[tile_list].reshape(WIN * TILE, HEADS, HEAD_DIM).astype(jnp.float32)
        value_window = value_tiles[tile_list].reshape(WIN * TILE, HEADS, HEAD_DIM).astype(jnp.float32)
        usable = jnp.repeat(jnp.arange(WIN, dtype=jnp.int32) < tile_count, TILE)
        scores = jnp.einsum("qhd,khd->hqk", tile_query.astype(jnp.float32), key_window) * inv_root
        scores = jnp.where(usable[None, None, :], scores, jnp.float32(-1e30))
        row_max = jnp.max(scores, axis=2, keepdims=True)
        raised = jnp.exp(scores - row_max)
        weights = (raised / jnp.sum(raised, axis=2, keepdims=True)).astype(jnp.bfloat16)
        result = jnp.einsum("hqk,khd->qhd", weights.astype(jnp.float32), value_window)
        return result.astype(jnp.bfloat16).reshape(TILE, D)

    attended = lax.map(one_tile, (query_tiles, windows, counts))
    return attended.reshape(TOKENS, D)
```

```python
import functools

import jax
import jax.numpy as jnp
from jax import lax
from jax.experimental import pallas as pl
from jax.experimental.pallas import tpu as pltpu
from jax.sharding import PartitionSpec as P

HEAD_DIM = 128
HT = 4
WT = 4
CORES = 2
FLAG_ROWS = 32
SUM_ROWS = 16
LOW = -3.0e38
EXPONENT_SCALE = HEAD_DIM ** (-0.5) * 1.4426950408889634
MESH = pl.DeviceIdType.MESH


def kernel(
    rows_of_tiles,
    frames,
    parts,
    windows,
    counts,
    queries,
    keys,
    values,
    out,
    kv,
    value_stage,
    query,
    flags,
    peak,
    total,
    out_stage,
    flag_recv,
    flag_send,
    deal_recv,
    query_recv,
    deal_send,
    chain_recv,
    chain_send,
    extra_recv,
    extra_send,
    out_recv,
    out_send,
):
    R = rows_of_tiles
    planes = frames // WT
    layers = planes // R
    rows = queries.shape[0]
    tile = rows * parts
    halves = parts // (2 * CORES)
    groups = WT * halves
    far = R + 1

    frame = lax.axis_index("frame")
    part = lax.axis_index("head")
    z, x = frame // WT, frame % WT
    layer, row = z // R, z % R
    y, k = part // CORES, part % CORES
    pair_half, p = y // 2, y % 2
    group = x * halves + pair_half
    inner, outer = 1 - k, k

    def reach(source, way):
        its_layer, its_row = source // R, source % R
        if way == 0:
            more_layers, more_rows = its_layer < layers - 1, its_row < R - 1
        else:
            more_layers, more_rows = its_layer > 0, its_row > 0
        rows_on = jnp.where(more_rows, 1, 0)
        return jnp.where(more_layers, R + rows_on, rows_on)

    def source_of(d, way):
        return z - d if way == 0 else z + d

    def travels(d, way, hop):
        source = source_of(d, way)
        inside = (source >= 0) & (source < planes)
        return inside & (hop <= reach(jnp.clip(source, 0, planes - 1), way))

    def steps_to(d, way):
        layer_step = jnp.where(d >= R - 1, -1, 0)
        row_step = jnp.where((d == 1) | (d == far), -1, jnp.where(d == R - 1, 1, 0))
        return (layer_step, row_step) if way == 0 else (-layer_step, -row_step)

    def used(d, way):
        layer_step, row_step = steps_to(d, way)
        there, its_row = layer + layer_step, row + row_step
        close = (d == 1) | (d >= R - 1)
        return close & (there >= 0) & (there < layers) & (its_row >= 0) & (its_row < R)

    def slot_of(d, way):
        return 1 + 2 * (d - 1) + way

    def column_of(unit):
        return jnp.where(unit == 2, 2 * p + k, 2 * k + unit)

    def head_of(unit):
        return 3 * group + jnp.where(unit == 2, 1, 2 * p)

    def lanes(index):
        return pl.ds(pl.multiple_of(index * HEAD_DIM, HEAD_DIM), HEAD_DIM)

    def own_rows(index):
        return pl.ds(pl.multiple_of(index * rows, rows), rows)

    def send_or_copy(mine, src, dst, send_sem, recv_sem, target):
        @pl.when(mine)
        def _():
            pltpu.make_async_copy(src, dst, recv_sem).start()

        @pl.when(jnp.logical_not(mine))
        def _():
            pltpu.make_async_remote_copy(
                src, dst, send_sem, recv_sem, device_id=target, device_id_type=MESH
            ).start()

    def await_bytes(ref, sem):
        pltpu.make_async_copy(ref, ref, sem).wait()

    barrier = pltpu.get_barrier_semaphore()
    plane_size = WT * parts

    def greet(i, carry):
        other_x = (x + i // parts) % WT
        other_part = (part + i % parts) % parts
        pl.semaphore_signal(
            barrier, inc=1, device_id=(z * WT + other_x, other_part), device_id_type=MESH
        )
        return carry

    lax.fori_loop(1, plane_size, greet, 0)

    @pl.when(z > 0)
    def _():
        pl.semaphore_signal(barrier, inc=1, device_id=(frame - WT, part), device_id_type=MESH)

    @pl.when(z < planes - 1)
    def _():
        pl.semaphore_signal(barrier, inc=1, device_id=(frame + WT, part), device_id_type=MESH)

    places = lax.broadcasted_iota(jnp.int32, (FLAG_ROWS, HEAD_DIM), 0)
    live_count = counts[0]

    def mark(j, live):
        listed = windows[0, j]
        place = (
            (listed // (R * WT) - layer + 1) * 9
            + (listed % (R * WT) // WT - row + 1) * 3
            + (listed % WT - x + 1)
        )
        place = jnp.where(j < live_count, place, FLAG_ROWS)
        return jnp.where(places == place, jnp.float32(1), live)

    flags[x] = lax.fori_loop(
        0, windows.shape[1], mark, jnp.zeros((FLAG_ROWS, HEAD_DIM), jnp.float32)
    )
    peak[...] = jnp.full(peak.shape, LOW, jnp.float32)
    total[...] = jnp.zeros(total.shape, jnp.float32)

    greeted = plane_size - 1 + jnp.where(z > 0, 1, 0) + jnp.where(z < planes - 1, 1, 0)
    pl.semaphore_wait(barrier, greeted)

    def dealt(head):
        if head == 1:
            return x // 2, x % 2, 2
        return head // 2, x // 2, x % 2

    def deal(head, tensors):
        to_p, to_core, unit = dealt(head)

        def one(i, carry):
            other = (group + i) % groups
            other_x, other_half = other // halves, other % halves
            other_part = (other_half * 2 + to_p) * CORES + to_core
            mine = (other == group) & (to_p == p) & (to_core == k)
            target = (z * WT + other_x, other_part)
            column = lanes(3 * other + head)
            for tensor in tensors:
                if tensor == 0:
                    src, dst, sem = keys, kv.at[0, unit, 0], deal_recv.at[unit]
                elif tensor == 1:
                    src, dst, sem = values, value_stage.at[unit], deal_recv.at[unit]
                else:
                    src, dst, sem = queries, query.at[unit], query_recv
                send_or_copy(
                    mine,
                    src.at[:, column],
                    dst.at[own_rows(part)],
                    deal_send.at[tensor, head],
                    sem,
                    target,
                )
            return carry

        lax.fori_loop(0, groups, one, 0)

    for head in (1, 0, 2):
        deal(head, (0, 1))
    for i in range(1, WT):
        pltpu.make_async_remote_copy(
            flags.at[x],
            flags.at[x],
            flag_send.at[i - 1],
            flag_recv.at[i - 1],
            device_id=(z * WT + (x + i) % WT, part),
            device_id_type=MESH,
        ).start()
    for head in (1, 0, 2):
        deal(head, (2,))

    def chain(d, way, unit):
        slot = jnp.where(d == 0, 0, slot_of(d, way))
        target = (frame + (WT if way == 0 else frames - WT)) % frames
        return pltpu.make_async_remote_copy(
            kv.at[slot, unit],
            kv.at[slot_of(d + 1, way), unit],
            chain_send.at[way, d, unit],
            chain_recv.at[way, d, unit],
            device_id=(target, part),
            device_id_type=MESH,
        )

    across = part + 1 - 2 * k
    has_partner = p != k
    partner = (pair_half * 2 + (1 - p)) * CORES + (1 - k)

    def extra(slot, which):
        unit = inner if which == 0 else 2
        return pltpu.make_async_remote_copy(
            kv.at[slot, unit],
            kv.at[slot, 3 + which],
            extra_send.at[slot, which],
            extra_recv.at[slot, which],
            device_id=(frame, partner if which == 2 else across),
            device_id_type=MESH,
        )

    def start_extras(slot, s):
        @pl.when(s == 0)
        def _():
            extra(slot, 1).start()

            @pl.when(has_partner)
            def _():
                extra(slot, 2).start()

        @pl.when(s == 1)
        def _():
            extra(slot, 0).start()

    def await_extras(slot, s):
        @pl.when(s == 1)
        def _():
            extra(slot, 1).wait_recv()

            @pl.when(has_partner)
            def _():
                extra(slot, 2).wait_recv()

        @pl.when(s == 2)
        def _():
            extra(slot, 0).wait_recv()

    def unit_at(s):
        return jnp.where(s == 0, 2, jnp.where(s == 1, inner, outer))

    def launch(s, carry):
        unit = unit_at(s)
        await_bytes(kv.at[0, unit], deal_recv.at[unit])
        for block in range(tile // HEAD_DIM):
            span = pl.ds(block * HEAD_DIM, HEAD_DIM)
            kv[0, unit, 1, span, :] = value_stage[unit, span, :].T
        for way in range(2):

            @pl.when(travels(0, way, 1))
            def _():
                chain(0, way, unit).start()

        start_extras(0, s)
        return carry

    lax.fori_loop(0, 3, launch, 0)
    await_bytes(query, query_recv)
    for i in range(1, WT):
        pltpu.make_async_remote_copy(
            flags.at[x],
            flags.at[(x - i) % WT],
            flag_send.at[i - 1],
            flag_recv.at[i - 1],
            device_id=(z * WT + (x + i) % WT, part),
            device_id_type=MESH,
        ).wait()

    beside = 1 - 2 * k
    summed = jnp.ones((SUM_ROWS, tile), jnp.bfloat16)

    def attend(i, d):
        on_q = jnp.where(
            (i == 0) | (i == 3) | (i == 4), 2, jnp.where((i == 2) | (i == 5), outer, inner)
        )
        on_kv = jnp.where(
            i <= 2,
            jnp.where(i == 0, 2, inner),
            jnp.where(
                i <= 4,
                jnp.where(i == 3, 4, jnp.where(has_partner, 5, 2)),
                jnp.where(i == 7, 3, outer),
            ),
        )
        shift = jnp.where(
            (i == 2) | (i == 3) | (i == 7), beside, jnp.where((i == 4) | (i == 6), -beside, 0)
        )
        column = column_of(on_q)
        one_query = query[on_q]

        def side(way):
            layer_step, row_step = steps_to(d, way)
            place = (layer_step + 1) * 9 + (row_step + 1) * 3 + shift + 1
            if way == 1:
                place = jnp.where(d == 0, FLAG_ROWS - 1, place)
            slot = jnp.where(used(d, way), slot_of(d, way), 0)
            flag = flags[column, pl.ds(place, 1), :]
            live = jnp.concatenate([flag] * (tile // HEAD_DIM), axis=1) > 0.5
            scores = lax.dot_general(
                kv[slot, on_kv, 0],
                one_query,
                (((1,), (1,)), ((), ())),
                preferred_element_type=jnp.float32,
            )
            top = jnp.where(live, jnp.max(scores, axis=0, keepdims=True), LOW)
            turned = kv[slot, on_kv, 1]
            turned = jnp.concatenate(
                [turned[b * HEAD_DIM : (b + 1) * HEAD_DIM] for b in range(tile // HEAD_DIM)], axis=1
            )
            return live, scores, top, jnp.concatenate([turned, summed], axis=0)

        sides = [side(0), side(1)]
        before = peak[on_q]
        now = jnp.maximum(before, jnp.maximum(sides[0][2], sides[1][2]))
        result = total[on_q] * jnp.exp2((before - now) * EXPONENT_SCALE)
        for live, scores, _, turned in sides:
            base = jnp.where(live, now, -LOW)
            weights = jnp.exp2((scores - base) * EXPONENT_SCALE).astype(jnp.bfloat16)
            result += jnp.dot(turned, weights, preferred_element_type=jnp.float32)
        peak[on_q] = now
        total[on_q] = result

    def step(t, carry):
        d, s = t // 3, t % 3
        unit = unit_at(s)

        @pl.when(d > 0)
        def _():
            for way in range(2):

                @pl.when(travels(d, way, d))
                def _():
                    chain(d - 1, way, unit).wait_recv()

                    @pl.when(travels(d, way, d + 1))
                    def _():
                        chain(d, way, unit).start()

                @pl.when(used(d, way))
                def _():
                    start_extras(slot_of(d, way), s)

        @pl.when(d == 0)
        def _():
            await_extras(0, s)

        @pl.when(d > 0)
        def _():
            for way in range(2):

                @pl.when(used(d, way))
                def _():
                    await_extras(slot_of(d, way), s)

        close = (d <= 1) | (d >= R - 1)
        first = jnp.where(s == 0, 0, jnp.where(s == 1, 1, 5))
        last = jnp.where(s == 0, 1, jnp.where(s == 1, 5, 8))

        def one(i, carry):
            attend(i, d)
            return carry

        lax.fori_loop(first, jnp.where(close, last, first), one, 0)
        return carry

    lax.fori_loop(0, 3 * (far + 1), step, 0)

    def deliver(s, carry):
        unit = unit_at(s)
        column = column_of(unit)
        sums = total[unit]
        scaled = sums[:HEAD_DIM] * (1.0 / sums[HEAD_DIM : HEAD_DIM + 1])
        out_stage[unit] = scaled.T.astype(jnp.bfloat16)

        def one(i, carry):
            to = (part + i) % parts
            send_or_copy(
                (to == part) & (column == x),
                out_stage.at[unit, own_rows(to)],
                out.at[:, lanes(head_of(unit))],
                out_send.at[unit],
                out_recv,
                (z * WT + column, to),
            )
            return carry

        lax.fori_loop(0, parts, one, 0)
        return carry

    lax.fori_loop(0, 3, deliver, 0)

    def settle_chain(t, carry):
        d, unit = t // 3, t % 3
        for way in range(2):

            @pl.when(travels(d, way, d + 1))
            def _():
                chain(d, way, unit).wait_send()

        return carry

    lax.fori_loop(0, 3 * far, settle_chain, 0)

    def settle_extras(slot):
        extra(slot, 0).wait_send()
        extra(slot, 1).wait_send()

        @pl.when(has_partner)
        def _():
            extra(slot, 2).wait_send()

    settle_extras(0)

    def settle(d, carry):
        for way in range(2):

            @pl.when(used(d, way))
            def _():
                settle_extras(slot_of(d, way))

        return carry

    lax.fori_loop(1, far + 1, settle, 0)

    def settle_sends(some_mine, count, sem):
        @pl.when(some_mine)
        def _():
            await_bytes(query.at[0, pl.ds(0, (count - 1) * rows)], sem)

        @pl.when(jnp.logical_not(some_mine))
        def _():
            await_bytes(query.at[0, pl.ds(0, count * rows)], sem)

    for head in range(3):
        to_p, to_core, _ = dealt(head)
        for tensor in range(3):
            settle_sends((to_p == p) & (to_core == k), groups, deal_send.at[tensor, head])
    for unit in range(3):
        settle_sends(column_of(unit) == x, parts, out_send.at[unit])
    await_bytes(out, out_recv)


def attention(rows_of_tiles, frames, parts, queries, keys, values, windows, counts):
    rows, width = queries.shape
    tile = rows * parts
    far = rows_of_tiles + 1
    slots = 1 + 2 * far
    any_space = pl.BlockSpec(memory_space=pl.ANY)
    scalars = pl.BlockSpec(memory_space=pltpu.SMEM)
    dma = pltpu.SemaphoreType.DMA
    return pl.pallas_call(
        functools.partial(kernel, rows_of_tiles, frames, parts),
        out_shape=jax.ShapeDtypeStruct((rows, width), jnp.bfloat16),
        in_specs=[scalars, scalars, any_space, any_space, any_space],
        out_specs=any_space,
        scratch_shapes=[
            pltpu.VMEM((slots, 6, 2, tile, HEAD_DIM), jnp.bfloat16),
            pltpu.VMEM((3, tile, HEAD_DIM), jnp.bfloat16),
            pltpu.VMEM((3, tile, HEAD_DIM), jnp.bfloat16),
            pltpu.VMEM((WT, FLAG_ROWS, HEAD_DIM), jnp.float32),
            pltpu.VMEM((3, 1, tile), jnp.float32),
            pltpu.VMEM((3, HEAD_DIM + SUM_ROWS, tile), jnp.float32),
            pltpu.VMEM((3, tile, HEAD_DIM), jnp.bfloat16),
            dma((WT - 1,)),
            dma((WT - 1,)),
            dma((3,)),
            dma,
            dma((3, 3)),
            dma((2, far, 3)),
            dma((2, far, 3)),
            dma((slots, 3)),
            dma((slots, 3)),
            dma,
            dma((3,)),
        ],
        compiler_params=pltpu.CompilerParams(
            collective_id=0, has_side_effects=True, vmem_limit_bytes=48 * 1024 * 1024
        ),
    )(windows, counts, queries, keys, values)


def solution(mesh):
    split = P(("frame", "head"), None)
    return jax.shard_map(
        functools.partial(attention, HT, mesh.shape["frame"], mesh.shape["head"]),
        mesh=mesh,
        in_specs=(split, split, split, P("frame", None), P("frame")),
        out_specs=split,
        check_vma=False,
    )
```

```python
import functools

import jax
import jax.numpy as jnp
from jax import lax
from jax.experimental import pallas as pl
from jax.experimental.pallas import tpu as pltpu
from jax.sharding import PartitionSpec as P

HEAD_DIM = 128
HT = 4
WT = 4
CORES = 2
FLAG_ROWS = 32
WINDOW = 27
SUM_ROWS = 16
LOW = -3.0e38
EXPONENT_SCALE = HEAD_DIM ** (-0.5) * 1.4426950408889634
MESH = pl.DeviceIdType.MESH


def kernel(
    rows_of_tiles,
    frames,
    parts,
    windows,
    counts,
    queries,
    keys,
    values,
    out,
    listed,
    live_count,
    kv,
    raw_keys,
    value_stage,
    query,
    flags,
    peak,
    total,
    out_stage,
    list_sem,
    flag_recv,
    flag_send,
    raw_recv,
    raw_send,
    key_recv,
    key_send,
    value_recv,
    value_send,
    query_recv,
    query_send,
    chain_recv,
    chain_send,
    extra_recv,
    extra_send,
    out_recv,
    out_send,
):
    R = rows_of_tiles
    planes = frames // WT
    layers = planes // R
    rows = queries.shape[0]
    tile = rows * parts
    blocks = tile // HEAD_DIM
    halves = parts // (2 * CORES)
    far = R + 1

    frame = lax.axis_index("frame")
    part = lax.axis_index("head")
    z, x = frame // WT, frame % WT
    layer, row = z // R, z % R
    y, k = part // CORES, part % CORES
    half, p = y // 2, y % 2
    inner, outer = 1 - k, k
    corner = z * WT

    def turned_by(index, by, size):
        moved = index + by
        return jnp.where(moved >= size, moved - size, moved)

    def loop(first, last, body):
        def one(i, carry):
            body(i)
            return carry

        lax.fori_loop(first, last, one, 0)

    lists = [
        pltpu.make_async_copy(windows, listed, list_sem.at[0]),
        pltpu.make_async_copy(counts, live_count, list_sem.at[1]),
    ]
    for copy in lists:
        copy.start()

    barrier = pltpu.get_barrier_semaphore()

    def greet(to):
        pl.semaphore_signal(barrier, inc=1, device_id=to, device_id_type=MESH)

    @pl.when(z > 0)
    def _():
        greet((frame - WT, part))

    @pl.when(z < planes - 1)
    def _():
        greet((frame + WT, part))

    other_parts = [turned_by(part, j, parts) if j else part for j in range(parts)]

    def greet_column(i):
        to = corner + turned_by(x, i, WT)
        for other in other_parts:
            greet((to, other))

    for other in other_parts[1:]:
        greet((frame, other))
    loop(1, WT, greet_column)
    greeted = WT * parts - 1 + jnp.where(z > 0, 1, 0) + jnp.where(z < planes - 1, 1, 0)
    pl.semaphore_wait(barrier, greeted)

    seen = [(z, layer, row), (planes - 1 - z, layers - 1 - layer, R - 1 - row)]

    def travels(d, way, hop):
        source = seen[way][0] - d
        its_row = seen[way][2] - d
        its_row = jnp.where(its_row < 0, its_row + R, its_row)
        its_row = jnp.where(its_row < 0, its_row + R, its_row)
        rows_on = its_row < R - 1
        far_enough = (hop <= R) | ((hop == far) & rows_on)
        short = (hop == 1) & rows_on
        more_layers = source < planes - R
        return (source >= 0) & ((more_layers & far_enough) | (jnp.logical_not(more_layers) & short))

    def steps_to(d, way):
        sign = 2 * way - 1
        row_step = jnp.where((d == 1) | (d == far), 1, jnp.where(d == R - 1, -1, 0))
        return sign * jnp.where(d >= R - 1, 1, 0), sign * row_step

    def used(d, way):
        _, its_layer, its_row = seen[way]
        near = (d == 1) & (its_row >= 1)
        back = (d == R - 1) & (its_row < R - 1)
        over = (d == R) | ((d == far) & (its_row >= 1))
        return near | ((its_layer >= 1) & (back | over))

    def slot_of(d, way):
        return 1 + 2 * (d - 1) + way

    def column_of(unit):
        return jnp.where(unit == 2, 2 * p + k, 2 * k + unit)

    def head_of(unit):
        return 3 * (x * halves + half) + jnp.where(unit == 2, 1, 2 * p)

    def lanes(index):
        return pl.ds(pl.multiple_of(index * HEAD_DIM, HEAD_DIM), HEAD_DIM)

    def own_rows(index):
        return pl.ds(pl.multiple_of(index * rows, rows), rows)

    def send(src, dst, send_sem, recv_sem, target):
        pltpu.make_async_remote_copy(
            src, dst, send_sem, recv_sem, device_id=target, device_id_type=MESH
        ).start()

    def send_or_copy(mine, src, dst, send_sem, recv_sem, target):
        @pl.when(mine)
        def _():
            pltpu.make_async_copy(src, dst, recv_sem).start()

        @pl.when(jnp.logical_not(mine))
        def _():
            send(src, dst, send_sem, recv_sem, target)

    def await_bytes(ref, sem):
        pltpu.make_async_copy(ref, ref, sem).wait()

    piece = halves * 3 * HEAD_DIM
    above = jnp.where(z == planes - 1, x, frame + WT)
    below = jnp.where(z == 0, frame + (frames - WT), frame - WT)

    def raw(way, i):
        columns = pl.ds(pl.multiple_of(turned_by(x, i, WT) * piece, HEAD_DIM), piece)
        return pltpu.make_async_remote_copy(
            keys.at[:, columns],
            raw_keys.at[way, :, columns],
            raw_send.at[way, i],
            raw_recv.at[way, i],
            device_id=(jnp.where(way == 0, above, below), part),
            device_id_type=MESH,
        )

    def start_raw(i):
        for way in range(2):

            @pl.when(travels(0, way, 1))
            def _():
                raw(way, i).start()

    loop(0, WT, start_raw)

    routes = [(0, x // 2, x % 2), (x // 2, x % 2, 2), (1, x // 2, x % 2)]
    mine = [(to_p == p) & (to_core == k) for to_p, to_core, _ in routes]
    mine_rows = own_rows(part)

    def deal_head(at, head, src, dst_of, send_sem_of, recv_sem_of):
        to_p, to_core, unit = routes[head]
        to_x = turned_by(x, at, WT)
        dst = dst_of(unit).at[mine_rows]
        first = 3 * halves * to_x + head
        for j in range(halves):
            other_half = turned_by(half, j, halves) if j else half
            copy = (
                src.at[:, lanes(first + 3 * other_half)],
                dst,
                send_sem_of(head),
                recv_sem_of(unit),
                (corner + to_x, (other_half * 2 + to_p) * CORES + to_core),
            )
            if j == 0:
                send_or_copy((at == 0) & mine[head], *copy)
            else:
                send(*copy)

    def deal(*how):
        for head in (1, 0, 2):
            loop(0, WT, lambda at: deal_head(at, head, *how))

    deal(values, value_stage.at.__getitem__, value_send.at.__getitem__, value_recv.at.__getitem__)

    def chain(d, way, unit, which):
        slot = jnp.where(d == 0, 0, slot_of(d, way))
        return pltpu.make_async_remote_copy(
            kv.at[slot, unit, which],
            kv.at[slot_of(d + 1, way), unit, which],
            chain_send.at[way, d, unit, which],
            chain_recv.at[way, d, unit, which],
            device_id=(jnp.where(way == 0, above, below), part),
            device_id_type=MESH,
        )

    across = part + 1 - 2 * k
    has_partner = p != k
    partner = (half * 2 + (1 - p)) * CORES + (1 - k)

    def extra(slot, which):
        unit = inner if which == 0 else 2
        return pltpu.make_async_remote_copy(
            kv.at[slot, unit],
            kv.at[slot, 3 + which],
            extra_send.at[slot, which],
            extra_recv.at[slot, which],
            device_id=(frame, partner if which == 2 else across),
            device_id_type=MESH,
        )

    def start_extras(slot, s):
        @pl.when(s == 0)
        def _():
            extra(slot, 1).start()

            @pl.when(has_partner)
            def _():
                extra(slot, 2).start()

        @pl.when(s == 1)
        def _():
            extra(slot, 0).start()

    def unit_at(s):
        return jnp.where(s == 0, 2, jnp.where(s == 1, inner, outer))

    def launch(s):
        unit = unit_at(s)
        await_bytes(value_stage.at[unit], value_recv.at[unit])

        def turn(block):
            span = pl.ds(pl.multiple_of(block * HEAD_DIM, HEAD_DIM), HEAD_DIM)
            kv[0, unit, 1, span, :] = value_stage[unit, span, :].T

        loop(0, blocks, turn)

        for way in range(2):

            @pl.when(travels(0, way, 1))
            def _():
                chain(0, way, unit, 1).start()

    def deal_piece(i):
        for way in range(2):

            @pl.when(travels(1, way, 1))
            def _():
                raw(way, i).wait_recv()
                for head in (1, 0, 2):
                    deal_head(
                        i,
                        head,
                        raw_keys.at[way],
                        lambda unit: kv.at[1 + way, unit, 0],
                        lambda head: key_send.at[1 + way, head],
                        lambda unit: key_recv.at[1 + way, unit],
                    )

        @pl.when(i < 3)
        def _():
            launch(i)

    loop(0, WT, deal_piece)

    for copy in lists:
        copy.wait()
    place = lax.broadcasted_iota(jnp.int32, (FLAG_ROWS, WINDOW), 0)
    layer_place = jnp.where(place >= 18, 2, jnp.where(place >= 9, 1, 0))
    rest = place - 9 * layer_place
    row_place = jnp.where(rest >= 6, 2, jnp.where(rest >= 3, 1, 0))
    rest = rest - 3 * row_place
    named = ((layer + layer_place - 1) * R + row + row_place - 1) * WT + x + rest - 1
    entry = lax.broadcasted_iota(jnp.int32, (FLAG_ROWS, WINDOW), 1)
    found = (named == listed[...]) & (entry < live_count[...]) & (place < WINDOW)
    found = jnp.max(jnp.where(found, jnp.float32(1), jnp.float32(0)), axis=1, keepdims=True)
    flags[x] = jnp.broadcast_to(found, (FLAG_ROWS, HEAD_DIM))

    def flag_copy(i, landing):
        return pltpu.make_async_remote_copy(
            flags.at[x],
            flags.at[landing],
            flag_send.at[i - 1],
            flag_recv.at[i - 1],
            device_id=(corner + turned_by(x, i, WT), part),
            device_id_type=MESH,
        )

    loop(1, WT, lambda i: flag_copy(i, x).start())

    def pass_keys(s):
        unit = unit_at(s)
        for way in range(2):

            @pl.when(travels(1, way, 1))
            def _():
                await_bytes(kv.at[1 + way, unit, 0], key_recv.at[1 + way, unit])

            @pl.when(travels(1, way, 2))
            def _():
                chain(1, way, unit, 0).start()

    def pass_values(s):
        unit = unit_at(s)
        for way in range(2):

            @pl.when(travels(1, way, 1))
            def _():
                chain(0, way, unit, 1).wait_recv()

            @pl.when(travels(1, way, 2))
            def _():
                chain(1, way, unit, 1).start()

            @pl.when(used(1, way))
            def _():
                start_extras(slot_of(1, way), s)

    loop(0, 3, pass_keys)
    loop(0, 3, pass_values)
    deal(queries, query.at.__getitem__, query_send.at.__getitem__, lambda unit: query_recv)
    deal(
        keys,
        lambda unit: kv.at[0, unit, 0],
        lambda head: key_send.at[0, head],
        lambda unit: key_recv.at[0, unit],
    )

    def clear(unit):
        peak[unit] = jnp.full(peak.shape[1:], LOW, jnp.float32)

        def clear_rows(i):
            span = pl.ds(pl.multiple_of(i * SUM_ROWS, SUM_ROWS), SUM_ROWS)
            total[unit, span, :] = jnp.zeros((SUM_ROWS, tile), jnp.float32)

        loop(0, HEAD_DIM // SUM_ROWS + 1, clear_rows)

    loop(0, 3, clear)
    loop(1, WT, lambda i: flag_copy(i, turned_by(x, WT - i, WT)).wait())

    beside = 1 - 2 * k
    summed = jnp.ones((SUM_ROWS, tile), jnp.bfloat16)

    def attend(i, d):
        on_q = jnp.where((i == 0) | (i == 3) | (i == 4), 2, jnp.where((i == 2) | (i == 6), outer, inner))
        on_kv = jnp.where(
            i <= 2,
            jnp.where(i == 0, 2, inner),
            jnp.where(
                i <= 4,
                jnp.where(i == 3, 4, jnp.where(has_partner, 5, 2)),
                jnp.where(i == 5, 3, outer),
            ),
        )
        shift = jnp.where(
            (i == 2) | (i == 3) | (i == 5), beside, jnp.where((i == 4) | (i == 7), -beside, 0)
        )
        column = column_of(on_q)
        one_query = query[on_q]

        def side(way):
            layer_step, row_step = steps_to(d, way)
            place = (layer_step + 1) * 9 + (row_step + 1) * 3 + shift + 1
            if way == 1:
                place = jnp.where(d == 0, FLAG_ROWS - 1, place)
            there = used(d, way)
            slot = jnp.where(there, slot_of(d, way), 0)
            at = jnp.where(there | (d == 0), on_kv, jnp.minimum(on_kv, 2))
            flag = flags[column, pl.ds(place, 1), :]
            live = jnp.concatenate([flag] * blocks, axis=1) > 0.5
            scores = lax.dot_general(
                kv[slot, at, 0],
                one_query,
                (((1,), (1,)), ((), ())),
                preferred_element_type=jnp.float32,
            )
            top = jnp.where(live, jnp.max(scores, axis=0, keepdims=True), LOW)
            turned = kv[slot, at, 1]
            turned = jnp.concatenate(
                [turned[b * HEAD_DIM : (b + 1) * HEAD_DIM] for b in range(blocks)], axis=1
            )
            return live, scores, top, jnp.concatenate([turned, summed], axis=0)

        sides = [side(0), side(1)]
        before = peak[on_q]
        now = jnp.maximum(before, jnp.maximum(sides[0][2], sides[1][2]))
        result = total[on_q] * jnp.exp2((before - now) * EXPONENT_SCALE)
        for live, scores, _, turned in sides:
            base = jnp.where(live, now, -LOW)
            weights = jnp.exp2((scores - base) * EXPONENT_SCALE).astype(jnp.bfloat16)
            result += jnp.dot(turned, weights, preferred_element_type=jnp.float32)
        peak[on_q] = now
        total[on_q] = result

    def deliver(unit):
        column = column_of(unit)
        sums = total[unit]
        scaled = sums[:HEAD_DIM] * (1.0 / sums[HEAD_DIM : HEAD_DIM + 1])
        out_stage[unit] = scaled.T.astype(jnp.bfloat16)

        target = corner + column
        head_lanes = lanes(head_of(unit))
        for i in range(parts):
            to = turned_by(part, i, parts) if i else part
            copy = (
                out_stage.at[unit, own_rows(to)],
                out.at[:, head_lanes],
                out_send.at[unit],
                out_recv,
                (target, to),
            )
            if i == 0:
                send_or_copy(column == x, *copy)
            else:
                send(*copy)

    def settle_chain(d, unit):
        for way in range(2):

            @pl.when(travels(d, way, d + 1))
            def _():
                @pl.when(d > 0)
                def _():
                    chain(d, way, unit, 0).wait_send()

                chain(d, way, unit, 1).wait_send()

    def settle_extras(slot, s):
        @pl.when(s == 0)
        def _():
            extra(slot, 1).wait_send()

            @pl.when(has_partner)
            def _():
                extra(slot, 2).wait_send()

        @pl.when(s == 1)
        def _():
            extra(slot, 0).wait_send()

    def settle_sends(some_mine, sem):
        @pl.when(some_mine)
        def _():
            await_bytes(query.at[0, pl.ds(0, tile - rows)], sem)

        @pl.when(jnp.logical_not(some_mine))
        def _():
            await_bytes(query.at[0], sem)

    def settle_deals():
        def settle_raw(i):
            for way in range(2):

                @pl.when(travels(0, way, 1))
                def _():
                    raw(way, i).wait_send()

        loop(0, WT, settle_raw)
        for head in range(3):
            settle_sends(mine[head], query_send.at[head])
            settle_sends(mine[head], value_send.at[head])
            settle_sends(mine[head], key_send.at[0, head])
            for way in range(2):

                @pl.when(travels(1, way, 1))
                def _():
                    settle_sends(mine[head], key_send.at[1 + way, head])

    def work(plane, s):
        def await_extra(which):
            @pl.when(plane == 0)
            def _():
                extra(0, which).wait_recv()

            for way in range(2):

                @pl.when(used(plane, way))
                def _():
                    extra(slot_of(plane, way), which).wait_recv()

        def one(i):
            @pl.when(i == 3)
            def _():
                await_extra(1)

                @pl.when(has_partner)
                def _():
                    await_extra(2)

            @pl.when(i == 5)
            def _():
                await_extra(0)

            attend(i, plane)

            @pl.when((plane == far) & ((i == 4) | (i >= 6)))
            def _():
                deliver(jnp.where(i == 4, 2, jnp.where(i == 6, outer, inner)))

        loop(jnp.where(s == 0, 0, jnp.where(s == 1, 1, 5)), jnp.where(s == 0, 1, jnp.where(s == 1, 5, 8)), one)

    def step(d, s):
        unit = unit_at(s)
        for way in range(2):
            on = travels(d, way, d + 1)

            @pl.when(travels(d, way, d))
            def _():
                for which in range(2):
                    chain(d - 1, way, unit, which).wait_recv()

                    @pl.when(on)
                    def _():
                        chain(d, way, unit, which).start()

            @pl.when(used(d, way))
            def _():
                start_extras(slot_of(d, way), s)

        settle_chain(d - 2, unit)

        @pl.when(d == 2)
        def _():
            @pl.when(s == 0)
            def _():
                await_bytes(query, query_recv)

            await_bytes(kv.at[0, unit, 0], key_recv.at[0, unit])
            start_extras(0, s)

        @pl.when(d == R)
        def _():
            settle_extras(0, s)

            @pl.when(s == 0)
            def _():
                settle_deals()

        for way in range(2):

            @pl.when(used(d - 1, way))
            def _():
                settle_extras(slot_of(d - 1, way), s)

        def turn(i):
            work(jnp.where(d == 2, 1, jnp.where((d == 3) & (i == 0), 0, d)), s)

        loop(0, jnp.where(d == 3, 2, 1), turn)

    def hop(d):
        loop(0, 3, lambda s: step(d, s))

    loop(2, far + 1, hop)

    def settle_last(s):
        settle_chain(far - 1, s)
        for way in range(2):

            @pl.when(used(far, way))
            def _():
                settle_extras(slot_of(far, way), s)

    loop(0, 3, settle_last)
    loop(0, 3, lambda unit: settle_sends(column_of(unit) == x, out_send.at[unit]))
    await_bytes(out, out_recv)


def attention(rows_of_tiles, frames, parts, queries, keys, values, windows, counts):
    rows, width = queries.shape
    tile = rows * parts
    far = rows_of_tiles + 1
    slots = 1 + 2 * far
    any_space = pl.BlockSpec(memory_space=pltpu.HBM)
    dma = pltpu.SemaphoreType.DMA
    return pl.pallas_call(
        functools.partial(kernel, rows_of_tiles, frames, parts),
        out_shape=pltpu.VMEM((rows, width), jnp.bfloat16),
        in_specs=[any_space] * 5,
        out_specs=pl.BlockSpec(memory_space=pltpu.VMEM),
        scratch_shapes=[
            pltpu.VMEM((1, WINDOW), jnp.int32),
            pltpu.VMEM((1, 1), jnp.int32),
            pltpu.VMEM((slots, 6, 2, tile, HEAD_DIM), jnp.bfloat16),
            pltpu.VMEM((2, rows, width), jnp.bfloat16),
            pltpu.VMEM((3, tile, HEAD_DIM), jnp.bfloat16),
            pltpu.VMEM((3, tile, HEAD_DIM), jnp.bfloat16),
            pltpu.VMEM((WT, FLAG_ROWS, HEAD_DIM), jnp.float32),
            pltpu.VMEM((3, 1, tile), jnp.float32),
            pltpu.VMEM((3, HEAD_DIM + SUM_ROWS, tile), jnp.float32),
            pltpu.VMEM((3, tile, HEAD_DIM), jnp.bfloat16),
            dma((2,)),
            dma((WT - 1,)),
            dma((WT - 1,)),
            dma((2, WT)),
            dma((2, WT)),
            dma((3, 3)),
            dma((3, 3)),
            dma((3,)),
            dma((3,)),
            dma,
            dma((3,)),
            dma((2, far, 3, 2)),
            dma((2, far, 3, 2)),
            dma((slots, 3)),
            dma((slots, 3)),
            dma,
            dma((3,)),
        ],
        compiler_params=pltpu.CompilerParams(
            collective_id=0, has_side_effects=True, vmem_limit_bytes=60 * 1024 * 1024
        ),
    )(windows, counts.reshape(1, 1), queries, keys, values)


def solution(mesh):
    split = P(("frame", "head"), None)
    return jax.shard_map(
        functools.partial(attention, HT, mesh.shape["frame"], mesh.shape["head"]),
        mesh=mesh,
        in_specs=(split, split, split, P("frame", None), P("frame")),
        out_specs=split,
        check_vma=False,
    )
```

```python
import functools

import jax
import jax.numpy as jnp
from jax import lax
from jax.experimental import pallas as pl
from jax.experimental.pallas import tpu as pltpu
from jax.sharding import PartitionSpec as P

HEAD_DIM = 128
HT = 4
WT = 4
CORES = 2
FLAG_ROWS = 32
WINDOW = 27
SUM_ROWS = 16
LOW = -3.0e38
EXPONENT_SCALE = HEAD_DIM ** (-0.5) * 1.4426950408889634
MESH = pl.DeviceIdType.MESH


def kernel(
    rows_of_tiles,
    frames,
    parts,
    windows,
    counts,
    queries,
    keys,
    values,
    out,
    listed,
    live_count,
    kv,
    raw_keys,
    value_stage,
    query,
    flags,
    peak,
    total,
    out_stage,
    list_sem,
    flag_recv,
    flag_send,
    raw_recv,
    raw_send,
    key_recv,
    key_send,
    value_recv,
    value_send,
    query_recv,
    query_send,
    chain_recv,
    chain_send,
    extra_recv,
    extra_send,
    out_recv,
    out_send,
):
    R = rows_of_tiles
    planes = frames // WT
    layers = planes // R
    rows = queries.shape[0]
    tile = rows * parts
    blocks = tile // HEAD_DIM
    halves = parts // (2 * CORES)
    far = R + 1

    frame = lax.axis_index("frame")
    part = lax.axis_index("head")
    z, x = frame // WT, frame % WT
    layer, row = z // R, z % R
    y, k = part // CORES, part % CORES
    half, p = y // 2, y % 2
    inner, outer = 1 - k, k
    corner = z * WT

    def turned_by(index, by, size):
        moved = index + by
        return jnp.where(moved >= size, moved - size, moved)

    def loop(first, last, body):
        def one(i, carry):
            body(i)
            return carry

        lax.fori_loop(first, last, one, 0)

    lists = [
        pltpu.make_async_copy(windows, listed, list_sem.at[0]),
        pltpu.make_async_copy(counts, live_count, list_sem.at[1]),
    ]
    for copy in lists:
        copy.start()

    barrier = pltpu.get_barrier_semaphore()

    def greet(to):
        pl.semaphore_signal(barrier, inc=1, device_id=to, device_id_type=MESH)

    @pl.when(z > 0)
    def _():
        greet((frame - WT, part))

    @pl.when(z < planes - 1)
    def _():
        greet((frame + WT, part))

    def far_first(t, way=0):
        beside = jnp.where((t == 1) == (way == 0), 1, 3)
        return jnp.where(t == 0, 2, jnp.where(t == WT - 1, 0, beside))

    part_steps = sorted(range(parts), key=lambda j: (-min(j, parts - j), j))
    other_parts = [turned_by(part, j, parts) if j else part for j in part_steps]

    def greet_column(t):
        to = corner + turned_by(x, far_first(t), WT)
        for other in other_parts:
            greet((to, other))

    loop(0, WT - 1, greet_column)
    for other in other_parts[:-1]:
        greet((frame, other))
    greeted = WT * parts - 1 + jnp.where(z > 0, 1, 0) + jnp.where(z < planes - 1, 1, 0)
    pl.semaphore_wait(barrier, greeted)

    seen = [(z, layer, row), (planes - 1 - z, layers - 1 - layer, R - 1 - row)]

    def travels(d, way, hop):
        source = seen[way][0] - d
        its_row = seen[way][2] - d
        its_row = jnp.where(its_row < 0, its_row + R, its_row)
        its_row = jnp.where(its_row < 0, its_row + R, its_row)
        rows_on = its_row < R - 1
        far_enough = (hop <= R) | ((hop == far) & rows_on)
        short = (hop == 1) & rows_on
        more_layers = source < planes - R
        return (source >= 0) & ((more_layers & far_enough) | (jnp.logical_not(more_layers) & short))

    def steps_to(d, way):
        sign = 2 * way - 1
        row_step = jnp.where((d == 1) | (d == far), 1, jnp.where(d == R - 1, -1, 0))
        return sign * jnp.where(d >= R - 1, 1, 0), sign * row_step

    def used(d, way):
        _, its_layer, its_row = seen[way]
        near = (d == 1) & (its_row >= 1)
        back = (d == R - 1) & (its_row < R - 1)
        over = (d == R) | ((d == far) & (its_row >= 1))
        return near | ((its_layer >= 1) & (back | over))

    def slot_of(d, way):
        return 1 + 2 * (d - 1) + way

    def column_of(unit):
        return jnp.where(unit == 2, 2 * p + k, 2 * k + unit)

    def head_of(unit):
        return 3 * (x * halves + half) + jnp.where(unit == 2, 1, 2 * p)

    def lanes(index):
        return pl.ds(pl.multiple_of(index * HEAD_DIM, HEAD_DIM), HEAD_DIM)

    def own_rows(index):
        return pl.ds(pl.multiple_of(index * rows, rows), rows)

    def send(src, dst, send_sem, recv_sem, target):
        pltpu.make_async_remote_copy(
            src, dst, send_sem, recv_sem, device_id=target, device_id_type=MESH
        ).start()

    def send_or_copy(mine, src, dst, send_sem, recv_sem, target):
        @pl.when(mine)
        def _():
            pltpu.make_async_copy(src, dst, recv_sem).start()

        @pl.when(jnp.logical_not(mine))
        def _():
            send(src, dst, send_sem, recv_sem, target)

    def await_bytes(ref, sem):
        pltpu.make_async_copy(ref, ref, sem).wait()

    piece = halves * 3 * HEAD_DIM
    above = jnp.where(z == planes - 1, x, frame + WT)
    below = jnp.where(z == 0, frame + (frames - WT), frame - WT)

    def raw(way, i):
        columns = pl.ds(
            pl.multiple_of(turned_by(x, far_first(i, way), WT) * piece, HEAD_DIM), piece
        )
        return pltpu.make_async_remote_copy(
            keys.at[:, columns],
            raw_keys.at[way, :, columns],
            raw_send.at[way, i],
            raw_recv.at[way, i],
            device_id=(jnp.where(way == 0, above, below), part),
            device_id_type=MESH,
        )

    def start_raw(i):
        for way in range(2):

            @pl.when(travels(0, way, 1))
            def _():
                raw(way, i).start()

    loop(0, WT, start_raw)

    routes = [(0, x // 2, x % 2), (x // 2, x % 2, 2), (1, x // 2, x % 2)]
    mine = [(to_p == p) & (to_core == k) for to_p, to_core, _ in routes]
    mine_rows = own_rows(part)

    def deal_head(at, head, src, dst_of, send_sem_of, recv_sem_of):
        to_p, to_core, unit = routes[head]
        to_x = turned_by(x, at, WT)
        dst = dst_of(unit).at[mine_rows]
        first = 3 * halves * to_x + head
        for j in range(halves):
            other_half = turned_by(half, j, halves) if j else half
            copy = (
                src.at[:, lanes(first + 3 * other_half)],
                dst,
                send_sem_of(head),
                recv_sem_of(unit),
                (corner + to_x, (other_half * 2 + to_p) * CORES + to_core),
            )
            if j == 0:
                send_or_copy((at == 0) & mine[head], *copy)
            else:
                send(*copy)

    def deal(*how):
        for head in (1, 0, 2):
            loop(0, WT, lambda t: deal_head(far_first(t), head, *how))

    deal(values, value_stage.at.__getitem__, value_send.at.__getitem__, value_recv.at.__getitem__)

    def chain(d, way, unit, which):
        slot = jnp.where(d == 0, 0, slot_of(d, way))
        return pltpu.make_async_remote_copy(
            kv.at[slot, unit, which],
            kv.at[slot_of(d + 1, way), unit, which],
            chain_send.at[way, d, unit, which],
            chain_recv.at[way, d, unit, which],
            device_id=(jnp.where(way == 0, above, below), part),
            device_id_type=MESH,
        )

    across = part + 1 - 2 * k
    has_partner = p != k
    partner = (half * 2 + (1 - p)) * CORES + (1 - k)

    def extra(slot, which):
        unit = inner if which == 0 else 2
        return pltpu.make_async_remote_copy(
            kv.at[slot, unit],
            kv.at[slot, 3 + which],
            extra_send.at[slot, which],
            extra_recv.at[slot, which],
            device_id=(frame, partner if which == 2 else across),
            device_id_type=MESH,
        )

    def start_extras(slot, s):
        @pl.when(s == 0)
        def _():
            extra(slot, 1).start()

            @pl.when(has_partner)
            def _():
                extra(slot, 2).start()

        @pl.when(s == 1)
        def _():
            extra(slot, 0).start()

    def unit_at(s):
        return jnp.where(s == 0, 2, jnp.where(s == 1, inner, outer))

    def launch(s):
        unit = unit_at(s)
        await_bytes(value_stage.at[unit], value_recv.at[unit])

        def turn(block):
            span = pl.ds(pl.multiple_of(block * HEAD_DIM, HEAD_DIM), HEAD_DIM)
            kv[0, unit, 1, span, :] = value_stage[unit, span, :].T

        loop(0, blocks, turn)

        for way in range(2):

            @pl.when(travels(0, way, 1))
            def _():
                chain(0, way, unit, 1).start()

    def deal_piece(i):
        for way in range(2):

            @pl.when(travels(1, way, 1))
            def _():
                raw(way, i).wait_recv()
                for head in (1, 0, 2):
                    deal_head(
                        far_first(i, way),
                        head,
                        raw_keys.at[way],
                        lambda unit: kv.at[1 + way, unit, 0],
                        lambda head: key_send.at[1 + way, head],
                        lambda unit: key_recv.at[1 + way, unit],
                    )

        @pl.when(i < 3)
        def _():
            launch(i)

    loop(0, WT, deal_piece)

    def pass_keys(s):
        unit = unit_at(s)
        for way in range(2):

            @pl.when(travels(1, way, 1))
            def _():
                await_bytes(kv.at[1 + way, unit, 0], key_recv.at[1 + way, unit])

            @pl.when(travels(1, way, 2))
            def _():
                chain(1, way, unit, 0).start()

    def pass_values(s):
        unit = unit_at(s)
        for way in range(2):

            @pl.when(travels(1, way, 1))
            def _():
                chain(0, way, unit, 1).wait_recv()

            @pl.when(travels(1, way, 2))
            def _():
                chain(1, way, unit, 1).start()

            @pl.when(used(1, way))
            def _():
                start_extras(slot_of(1, way), s)

    loop(0, 3, pass_keys)

    for copy in lists:
        copy.wait()
    place = lax.broadcasted_iota(jnp.int32, (FLAG_ROWS, WINDOW), 0)
    layer_place = jnp.where(place >= 18, 2, jnp.where(place >= 9, 1, 0))
    rest = place - 9 * layer_place
    row_place = jnp.where(rest >= 6, 2, jnp.where(rest >= 3, 1, 0))
    rest = rest - 3 * row_place
    named = ((layer + layer_place - 1) * R + row + row_place - 1) * WT + x + rest - 1
    entry = lax.broadcasted_iota(jnp.int32, (FLAG_ROWS, WINDOW), 1)
    found = (named == listed[...]) & (entry < live_count[...]) & (place < WINDOW)
    found = jnp.max(jnp.where(found, jnp.float32(1), jnp.float32(0)), axis=1, keepdims=True)
    flags[x] = jnp.broadcast_to(found, (FLAG_ROWS, HEAD_DIM))

    def flag_copy(i, landing):
        return pltpu.make_async_remote_copy(
            flags.at[x],
            flags.at[landing],
            flag_send.at[i - 1],
            flag_recv.at[i - 1],
            device_id=(corner + turned_by(x, i, WT), part),
            device_id_type=MESH,
        )

    loop(1, WT, lambda i: flag_copy(i, x).start())

    loop(0, 3, pass_values)
    deal(queries, query.at.__getitem__, query_send.at.__getitem__, lambda unit: query_recv)
    deal(
        keys,
        lambda unit: kv.at[0, unit, 0],
        lambda head: key_send.at[0, head],
        lambda unit: key_recv.at[0, unit],
    )

    def clear(unit):
        peak[unit] = jnp.full(peak.shape[1:], LOW, jnp.float32)

        def clear_rows(i):
            span = pl.ds(pl.multiple_of(i * SUM_ROWS, SUM_ROWS), SUM_ROWS)
            total[unit, span, :] = jnp.zeros((SUM_ROWS, tile), jnp.float32)

        loop(0, HEAD_DIM // SUM_ROWS + 1, clear_rows)

    loop(0, 3, clear)
    loop(1, WT, lambda i: flag_copy(i, turned_by(x, WT - i, WT)).wait())

    beside = 1 - 2 * k
    summed = jnp.ones((SUM_ROWS, tile), jnp.bfloat16)

    def attend(i, d):
        on_q = jnp.where((i == 0) | (i == 3) | (i == 4), 2, jnp.where((i == 2) | (i == 6), outer, inner))
        on_kv = jnp.where(
            i <= 2,
            jnp.where(i == 0, 2, inner),
            jnp.where(
                i <= 4,
                jnp.where(i == 3, 4, jnp.where(has_partner, 5, 2)),
                jnp.where(i == 5, 3, outer),
            ),
        )
        shift = jnp.where(
            (i == 2) | (i == 3) | (i == 5), beside, jnp.where((i == 4) | (i == 7), -beside, 0)
        )
        column = column_of(on_q)
        one_query = query[on_q]

        def side(way):
            layer_step, row_step = steps_to(d, way)
            place = (layer_step + 1) * 9 + (row_step + 1) * 3 + shift + 1
            if way == 1:
                place = jnp.where(d == 0, FLAG_ROWS - 1, place)
            there = used(d, way)
            slot = jnp.where(there, slot_of(d, way), 0)
            at = jnp.where(there | (d == 0), on_kv, jnp.minimum(on_kv, 2))
            flag = flags[column, pl.ds(place, 1), :]
            live = jnp.concatenate([flag] * blocks, axis=1) > 0.5
            scores = lax.dot_general(
                kv[slot, at, 0],
                one_query,
                (((1,), (1,)), ((), ())),
                preferred_element_type=jnp.float32,
            )
            top = jnp.where(live, jnp.max(scores, axis=0, keepdims=True), LOW)
            turned = kv[slot, at, 1]
            turned = jnp.concatenate(
                [turned[b * HEAD_DIM : (b + 1) * HEAD_DIM] for b in range(blocks)], axis=1
            )
            return live, scores, top, jnp.concatenate([turned, summed], axis=0)

        sides = [side(0), side(1)]
        before = peak[on_q]
        now = jnp.maximum(before, jnp.maximum(sides[0][2], sides[1][2]))
        result = total[on_q] * jnp.exp2((before - now) * EXPONENT_SCALE)
        for live, scores, _, turned in sides:
            base = jnp.where(live, now, -LOW)
            weights = jnp.exp2((scores - base) * EXPONENT_SCALE).astype(jnp.bfloat16)
            result += jnp.dot(turned, weights, preferred_element_type=jnp.float32)
        peak[on_q] = now
        total[on_q] = result

    def deliver(unit):
        column = column_of(unit)
        sums = total[unit]
        scaled = sums[:HEAD_DIM] * (1.0 / sums[HEAD_DIM : HEAD_DIM + 1])
        out_stage[unit] = scaled.T.astype(jnp.bfloat16)

        target = corner + column
        head_lanes = lanes(head_of(unit))
        for to in other_parts:
            copy = (
                out_stage.at[unit, own_rows(to)],
                out.at[:, head_lanes],
                out_send.at[unit],
                out_recv,
                (target, to),
            )
            if to is part:
                send_or_copy(column == x, *copy)
            else:
                send(*copy)

    def settle_chain(d, unit):
        for way in range(2):

            @pl.when(travels(d, way, d + 1))
            def _():
                @pl.when(d > 0)
                def _():
                    chain(d, way, unit, 0).wait_send()

                chain(d, way, unit, 1).wait_send()

    def settle_extras(slot, s):
        @pl.when(s == 0)
        def _():
            extra(slot, 1).wait_send()

            @pl.when(has_partner)
            def _():
                extra(slot, 2).wait_send()

        @pl.when(s == 1)
        def _():
            extra(slot, 0).wait_send()

    def settle_sends(some_mine, sem):
        @pl.when(some_mine)
        def _():
            await_bytes(query.at[0, pl.ds(0, tile - rows)], sem)

        @pl.when(jnp.logical_not(some_mine))
        def _():
            await_bytes(query.at[0], sem)

    def settle_deals():
        def settle_raw(i):
            for way in range(2):

                @pl.when(travels(0, way, 1))
                def _():
                    raw(way, i).wait_send()

        loop(0, WT, settle_raw)
        for head in range(3):
            settle_sends(mine[head], query_send.at[head])
            settle_sends(mine[head], value_send.at[head])
            settle_sends(mine[head], key_send.at[0, head])
            for way in range(2):

                @pl.when(travels(1, way, 1))
                def _():
                    settle_sends(mine[head], key_send.at[1 + way, head])

    def work(plane, place, idle):
        def await_extra(which):
            @pl.when(plane == 0)
            def _():
                extra(0, which).wait_recv()

            for way in range(2):

                @pl.when(used(plane, way))
                def _():
                    extra(slot_of(plane, way), which).wait_recv()

        def one(i):
            @pl.when(i == 3)
            def _():
                await_extra(1)

                @pl.when(has_partner)
                def _():
                    await_extra(2)

            @pl.when(i == 5)
            def _():
                await_extra(0)

            attend(i, plane)

            @pl.when((plane == far) & ((i == 4) | (i >= 6)))
            def _():
                deliver(jnp.where(i == 4, 2, jnp.where(i == 6, outer, inner)))

        first = jnp.where(place == 0, 0, jnp.where(place == 1, 1, place + 3))
        last = jnp.where(place == 0, 1, jnp.where(place == 1, 5, 2 * place + 2))
        loop(first, jnp.where(idle, first, last), one)

    def arrive(d, s, unit):
        for way in range(2):
            on = travels(d, way, d + 1)

            @pl.when(travels(d, way, d))
            def _():
                for which in range(2):
                    chain(d - 1, way, unit, which).wait_recv()

                    @pl.when(on)
                    def _():
                        chain(d, way, unit, which).start()

            @pl.when(used(d, way))
            def _():
                start_extras(slot_of(d, way), s)

        settle_chain(d - 2, unit)

        @pl.when(d == R)
        def _():
            settle_extras(0, s)

            @pl.when(s == 0)
            def _():
                settle_deals()

        for way in range(2):

            @pl.when(used(d - 1, way))
            def _():
                settle_extras(slot_of(d - 1, way), s)

    def step(d, place):
        s = jnp.where(place == 3, 2, place)
        unit = unit_at(s)

        def phase(turn):
            @pl.when((turn == 0) & (d == 2) & (place != 2))
            def _():
                @pl.when(s == 0)
                def _():
                    await_bytes(query, query_recv)

                await_bytes(kv.at[0, unit, 0], key_recv.at[0, unit])
                start_extras(0, s)

            @pl.when((turn == 1) & (place != 2))
            def _():
                arrive(d, s, unit)

            idle = ((turn == 0) & (d > 3)) | ((turn == 1) & (d == 2))
            work(jnp.where(turn == 1, d, jnp.where(d == 2, 1, 0)), place, idle)

        loop(0, 2, phase)

    def hop(d):
        loop(0, 4, lambda place: step(d, place))

    loop(2, far + 1, hop)

    def settle_last(s):
        settle_chain(far - 1, s)
        for way in range(2):

            @pl.when(used(far, way))
            def _():
                settle_extras(slot_of(far, way), s)

    loop(0, 3, settle_last)
    loop(0, 3, lambda unit: settle_sends(column_of(unit) == x, out_send.at[unit]))
    await_bytes(out, out_recv)


def attention(rows_of_tiles, frames, parts, queries, keys, values, windows, counts):
    rows, width = queries.shape
    tile = rows * parts
    far = rows_of_tiles + 1
    slots = 1 + 2 * far
    any_space = pl.BlockSpec(memory_space=pltpu.HBM)
    dma = pltpu.SemaphoreType.DMA
    return pl.pallas_call(
        functools.partial(kernel, rows_of_tiles, frames, parts),
        out_shape=pltpu.VMEM((rows, width), jnp.bfloat16),
        in_specs=[any_space] * 5,
        out_specs=pl.BlockSpec(memory_space=pltpu.VMEM),
        scratch_shapes=[
            pltpu.VMEM((1, WINDOW), jnp.int32),
            pltpu.VMEM((1, 1), jnp.int32),
            pltpu.VMEM((slots, 6, 2, tile, HEAD_DIM), jnp.bfloat16),
            pltpu.VMEM((2, rows, width), jnp.bfloat16),
            pltpu.VMEM((3, tile, HEAD_DIM), jnp.bfloat16),
            pltpu.VMEM((3, tile, HEAD_DIM), jnp.bfloat16),
            pltpu.VMEM((WT, FLAG_ROWS, HEAD_DIM), jnp.float32),
            pltpu.VMEM((3, 1, tile), jnp.float32),
            pltpu.VMEM((3, HEAD_DIM + SUM_ROWS, tile), jnp.float32),
            pltpu.VMEM((3, tile, HEAD_DIM), jnp.bfloat16),
            dma((2,)),
            dma((WT - 1,)),
            dma((WT - 1,)),
            dma((2, WT)),
            dma((2, WT)),
            dma((3, 3)),
            dma((3, 3)),
            dma((3,)),
            dma((3,)),
            dma,
            dma((3,)),
            dma((2, far, 3, 2)),
            dma((2, far, 3, 2)),
            dma((slots, 3)),
            dma((slots, 3)),
            dma,
            dma((3,)),
        ],
        compiler_params=pltpu.CompilerParams(
            collective_id=0, has_side_effects=True, vmem_limit_bytes=60 * 1024 * 1024
        ),
    )(windows, counts.reshape(1, 1), queries, keys, values)


def solution(mesh):
    split = P(("frame", "head"), None)
    return jax.shard_map(
        functools.partial(attention, HT, mesh.shape["frame"], mesh.shape["head"]),
        mesh=mesh,
        in_specs=(split, split, split, P("frame", None), P("frame")),
        out_specs=split,
        check_vma=False,
    )
```

```python
import functools

import jax
import jax.numpy as jnp
from jax import lax
from jax.experimental import pallas as pl
from jax.experimental.pallas import tpu as pltpu
from jax.sharding import PartitionSpec as P

HEAD_DIM = 128
HT = 4
WT = 4
CORES = 2
FLAG_ROWS = 32
WINDOW = 27
SUM_ROWS = 16
LOW = -3.0e38
EXPONENT_SCALE = HEAD_DIM ** (-0.5) * 1.4426950408889634
MESH = pl.DeviceIdType.MESH


def kernel(
    rows_of_tiles,
    frames,
    parts,
    windows,
    counts,
    queries,
    keys,
    values,
    out,
    listed,
    live_count,
    kv,
    raw_keys,
    value_stage,
    query,
    flags,
    peak,
    total,
    out_stage,
    list_sem,
    flag_recv,
    flag_send,
    raw_recv,
    raw_send,
    key_recv,
    key_send,
    value_recv,
    value_send,
    query_recv,
    query_send,
    chain_recv,
    chain_send,
    extra_recv,
    extra_send,
    out_recv,
    out_send,
):
    R = rows_of_tiles
    planes = frames // WT
    layers = planes // R
    rows = queries.shape[0]
    tile = rows * parts
    blocks = tile // HEAD_DIM
    halves = parts // (2 * CORES)
    far = R + 1

    frame = lax.axis_index("frame")
    part = lax.axis_index("head")
    z, x = frame // WT, frame % WT
    layer, row = z // R, z % R
    y, k = part // CORES, part % CORES
    half, p = y // 2, y % 2
    inner, outer = 1 - k, k
    corner = z * WT

    def turned_by(index, by, size):
        moved = index + by
        return jnp.where(moved >= size, moved - size, moved)

    def loop(first, last, body):
        def one(i, carry):
            body(i)
            return carry

        lax.fori_loop(first, last, one, 0)

    lists = [
        pltpu.make_async_copy(windows, listed, list_sem.at[0]),
        pltpu.make_async_copy(counts, live_count, list_sem.at[1]),
    ]
    for copy in lists:
        copy.start()

    barrier = pltpu.get_barrier_semaphore()

    def greet(to):
        pl.semaphore_signal(barrier, inc=1, device_id=to, device_id_type=MESH)

    @pl.when(z > 0)
    def _():
        greet((frame - WT, part))

    @pl.when(z < planes - 1)
    def _():
        greet((frame + WT, part))

    def far_first(t, way=0):
        beside = jnp.where((t == 1) == (way == 0), 1, 3)
        return jnp.where(t == 0, 2, jnp.where(t == WT - 1, 0, beside))

    part_steps = sorted(range(parts), key=lambda j: (-min(j, parts - j), j))
    other_parts = [turned_by(part, j, parts) if j else part for j in part_steps]

    def greet_column(t):
        to = corner + turned_by(x, far_first(t), WT)
        for other in other_parts:
            greet((to, other))

    loop(0, WT - 1, greet_column)
    for other in other_parts[:-1]:
        greet((frame, other))
    greeted = WT * parts - 1 + jnp.where(z > 0, 1, 0) + jnp.where(z < planes - 1, 1, 0)
    pl.semaphore_wait(barrier, greeted)

    seen = [(z, layer, row), (planes - 1 - z, layers - 1 - layer, R - 1 - row)]

    def travels(d, way, hop):
        source = seen[way][0] - d
        its_row = seen[way][2] - d
        its_row = jnp.where(its_row < 0, its_row + R, its_row)
        its_row = jnp.where(its_row < 0, its_row + R, its_row)
        rows_on = its_row < R - 1
        far_enough = (hop <= R) | ((hop == far) & rows_on)
        short = (hop == 1) & rows_on
        more_layers = source < planes - R
        return (source >= 0) & ((more_layers & far_enough) | (jnp.logical_not(more_layers) & short))

    def steps_to(d, way):
        sign = 2 * way - 1
        row_step = jnp.where((d == 1) | (d == far), 1, jnp.where(d == R - 1, -1, 0))
        return sign * jnp.where(d >= R - 1, 1, 0), sign * row_step

    def used(d, way):
        _, its_layer, its_row = seen[way]
        near = (d == 1) & (its_row >= 1)
        back = (d == R - 1) & (its_row < R - 1)
        over = (d == R) | ((d == far) & (its_row >= 1))
        return near | ((its_layer >= 1) & (back | over))

    def slot_of(d, way):
        return 1 + 2 * (d - 1) + way

    def column_of(unit):
        return jnp.where(unit == 2, 2 * p + k, 2 * k + unit)

    def head_of(unit):
        return 3 * (x * halves + half) + jnp.where(unit == 2, 1, 2 * p)

    def lanes(index):
        return pl.ds(pl.multiple_of(index * HEAD_DIM, HEAD_DIM), HEAD_DIM)

    def own_rows(index):
        return pl.ds(pl.multiple_of(index * rows, rows), rows)

    def send(src, dst, send_sem, recv_sem, target):
        pltpu.make_async_remote_copy(
            src, dst, send_sem, recv_sem, device_id=target, device_id_type=MESH
        ).start()

    def send_or_copy(mine, src, dst, send_sem, recv_sem, target):
        @pl.when(mine)
        def _():
            pltpu.make_async_copy(src, dst, recv_sem).start()

        @pl.when(jnp.logical_not(mine))
        def _():
            send(src, dst, send_sem, recv_sem, target)

    def await_bytes(ref, sem):
        pltpu.make_async_copy(ref, ref, sem).wait()

    piece = halves * 3 * HEAD_DIM
    above = jnp.where(z == planes - 1, x, frame + WT)
    below = jnp.where(z == 0, frame + (frames - WT), frame - WT)

    def raw(way, i):
        columns = pl.ds(
            pl.multiple_of(turned_by(x, far_first(i, way), WT) * piece, HEAD_DIM), piece
        )
        return pltpu.make_async_remote_copy(
            keys.at[:, columns],
            raw_keys.at[way, :, columns],
            raw_send.at[way, i],
            raw_recv.at[way, i],
            device_id=(jnp.where(way == 0, above, below), part),
            device_id_type=MESH,
        )

    def start_raw(i):
        for way in range(2):

            @pl.when(travels(0, way, 1))
            def _():
                raw(way, i).start()

    loop(0, WT, start_raw)

    routes = [(0, x // 2, x % 2), (x // 2, x % 2, 2), (1, x // 2, x % 2)]
    mine = [(to_p == p) & (to_core == k) for to_p, to_core, _ in routes]
    mine_rows = own_rows(part)

    def deal_head(at, head, src, dst_of, send_sem_of, recv_sem_of):
        to_p, to_core, unit = routes[head]
        to_x = turned_by(x, at, WT)
        dst = dst_of(unit).at[mine_rows]
        first = 3 * halves * to_x + head
        for j in range(halves):
            other_half = turned_by(half, j, halves) if j else half
            copy = (
                src.at[:, lanes(first + 3 * other_half)],
                dst,
                send_sem_of(head),
                recv_sem_of(unit),
                (corner + to_x, (other_half * 2 + to_p) * CORES + to_core),
            )
            if j == 0:
                send_or_copy((at == 0) & mine[head], *copy)
            else:
                send(*copy)

    def deal(*how):
        for head in (1, 0, 2):
            loop(0, WT, lambda t: deal_head(far_first(t), head, *how))

    deal(values, value_stage.at.__getitem__, value_send.at.__getitem__, value_recv.at.__getitem__)

    def chain(d, way, unit, which):
        slot = jnp.where(d == 0, 0, slot_of(d, way))
        return pltpu.make_async_remote_copy(
            kv.at[slot, unit, which],
            kv.at[slot_of(d + 1, way), unit, which],
            chain_send.at[way, d, unit, which],
            chain_recv.at[way, d, unit, which],
            device_id=(jnp.where(way == 0, above, below), part),
            device_id_type=MESH,
        )

    across = part + 1 - 2 * k
    has_partner = p != k
    partner = (half * 2 + (1 - p)) * CORES + (1 - k)

    def extra(slot, which):
        unit = inner if which == 0 else 2
        return pltpu.make_async_remote_copy(
            kv.at[slot, unit],
            kv.at[slot, 3 + which],
            extra_send.at[slot, which],
            extra_recv.at[slot, which],
            device_id=(frame, partner if which == 2 else across),
            device_id_type=MESH,
        )

    def start_extras(slot, s):
        @pl.when(s == 0)
        def _():
            extra(slot, 1).start()

            @pl.when(has_partner)
            def _():
                extra(slot, 2).start()

        @pl.when(s == 1)
        def _():
            extra(slot, 0).start()

    def unit_at(s):
        return jnp.where(s == 0, 2, jnp.where(s == 1, inner, outer))

    def launch(s):
        unit = unit_at(s)
        await_bytes(value_stage.at[unit], value_recv.at[unit])

        def turn(block):
            span = pl.ds(pl.multiple_of(block * HEAD_DIM, HEAD_DIM), HEAD_DIM)
            kv[0, unit, 1, span, :] = value_stage[unit, span, :].T

        loop(0, blocks, turn)

        for way in range(2):

            @pl.when(travels(0, way, 1))
            def _():
                chain(0, way, unit, 1).start()

    def deal_piece(i):
        for way in range(2):

            @pl.when(travels(1, way, 1))
            def _():
                raw(way, i).wait_recv()
                for head in (1, 0, 2):
                    deal_head(
                        far_first(i, way),
                        head,
                        raw_keys.at[way],
                        lambda unit: kv.at[1 + way, unit, 0],
                        lambda head: key_send.at[1 + way, head],
                        lambda unit: key_recv.at[1 + way, unit],
                    )

        @pl.when(i < 3)
        def _():
            launch(i)

    loop(0, WT, deal_piece)

    def pass_keys(s):
        unit = unit_at(s)
        for way in range(2):

            @pl.when(travels(1, way, 1))
            def _():
                await_bytes(kv.at[1 + way, unit, 0], key_recv.at[1 + way, unit])

            @pl.when(travels(1, way, 2))
            def _():
                chain(1, way, unit, 0).start()

    def pass_values(s):
        unit = unit_at(s)
        for way in range(2):

            @pl.when(travels(1, way, 1))
            def _():
                chain(0, way, unit, 1).wait_recv()

            @pl.when(travels(1, way, 2))
            def _():
                chain(1, way, unit, 1).start()

            @pl.when(used(1, way))
            def _():
                start_extras(slot_of(1, way), s)

    loop(0, 3, pass_keys)

    for copy in lists:
        copy.wait()
    place = lax.broadcasted_iota(jnp.int32, (FLAG_ROWS, WINDOW), 0)
    layer_place = jnp.where(place >= 18, 2, jnp.where(place >= 9, 1, 0))
    rest = place - 9 * layer_place
    row_place = jnp.where(rest >= 6, 2, jnp.where(rest >= 3, 1, 0))
    rest = rest - 3 * row_place
    named = ((layer + layer_place - 1) * R + row + row_place - 1) * WT + x + rest - 1
    entry = lax.broadcasted_iota(jnp.int32, (FLAG_ROWS, WINDOW), 1)
    found = (named == listed[...]) & (entry < live_count[...]) & (place < WINDOW)
    found = jnp.max(jnp.where(found, jnp.float32(1), jnp.float32(0)), axis=1, keepdims=True)
    flags[x] = jnp.broadcast_to(found, (FLAG_ROWS, HEAD_DIM))

    def flag_copy(i, landing):
        return pltpu.make_async_remote_copy(
            flags.at[x],
            flags.at[landing],
            flag_send.at[i - 1],
            flag_recv.at[i - 1],
            device_id=(corner + turned_by(x, i, WT), part),
            device_id_type=MESH,
        )

    loop(1, WT, lambda i: flag_copy(i, x).start())

    loop(0, 3, pass_values)
    deal(queries, query.at.__getitem__, query_send.at.__getitem__, lambda unit: query_recv)
    deal(
        keys,
        lambda unit: kv.at[0, unit, 0],
        lambda head: key_send.at[0, head],
        lambda unit: key_recv.at[0, unit],
    )

    def clear(unit):
        peak[unit] = jnp.full(peak.shape[1:], LOW, jnp.float32)

        def clear_rows(i):
            span = pl.ds(pl.multiple_of(i * SUM_ROWS, SUM_ROWS), SUM_ROWS)
            total[unit, span, :] = jnp.zeros((SUM_ROWS, tile), jnp.float32)

        loop(0, HEAD_DIM // SUM_ROWS + 1, clear_rows)

    loop(0, 3, clear)
    loop(1, WT, lambda i: flag_copy(i, turned_by(x, WT - i, WT)).wait())

    beside = 1 - 2 * k
    summed = jnp.ones((SUM_ROWS, tile), jnp.bfloat16)

    def attend(i, d, ways):
        on_q = jnp.where((i == 0) | (i == 3) | (i == 4), 2, jnp.where((i == 2) | (i == 6), outer, inner))
        on_kv = jnp.where(
            i <= 2,
            jnp.where(i == 0, 2, inner),
            jnp.where(
                i <= 4,
                jnp.where(i == 3, 4, jnp.where(has_partner, 5, 2)),
                jnp.where(i == 5, 3, outer),
            ),
        )
        shift = jnp.where(
            (i == 2) | (i == 3) | (i == 5), beside, jnp.where((i == 4) | (i == 7), -beside, 0)
        )
        column = column_of(on_q)
        one_query = query[on_q]

        def side(way):
            layer_step, row_step = steps_to(d, way)
            place = (layer_step + 1) * 9 + (row_step + 1) * 3 + shift + 1
            there = used(d, way)
            slot = jnp.where(there, slot_of(d, way), 0)
            at = jnp.where(there | (d == 0), on_kv, jnp.minimum(on_kv, 2))
            flag = flags[column, pl.ds(place, 1), :]
            live = jnp.concatenate([flag] * blocks, axis=1) > 0.5
            scores = lax.dot_general(
                kv[slot, at, 0],
                one_query,
                (((1,), (1,)), ((), ())),
                preferred_element_type=jnp.float32,
            )
            top = jnp.where(live, jnp.max(scores, axis=0, keepdims=True), LOW)
            turned = kv[slot, at, 1]
            turned = jnp.concatenate(
                [turned[b * HEAD_DIM : (b + 1) * HEAD_DIM] for b in range(blocks)], axis=1
            )
            return live, scores, top, jnp.concatenate([turned, summed], axis=0)

        sides = [side(way) for way in ways]
        before = peak[on_q]
        now = before
        for _, _, top, _ in sides:
            now = jnp.maximum(now, top)
        result = total[on_q] * jnp.exp2((before - now) * EXPONENT_SCALE)
        for live, scores, _, turned in sides:
            base = jnp.where(live, now, -LOW)
            weights = jnp.exp2((scores - base) * EXPONENT_SCALE).astype(jnp.bfloat16)
            result += jnp.dot(turned, weights, preferred_element_type=jnp.float32)
        peak[on_q] = now
        total[on_q] = result

    def deliver(unit):
        column = column_of(unit)
        sums = total[unit]
        scaled = sums[:HEAD_DIM] * (1.0 / sums[HEAD_DIM : HEAD_DIM + 1])
        out_stage[unit] = scaled.T.astype(jnp.bfloat16)

        target = corner + column
        head_lanes = lanes(head_of(unit))
        for to in other_parts:
            copy = (
                out_stage.at[unit, own_rows(to)],
                out.at[:, head_lanes],
                out_send.at[unit],
                out_recv,
                (target, to),
            )
            if to is part:
                send_or_copy(column == x, *copy)
            else:
                send(*copy)

    def settle_chain(d, unit):
        for way in range(2):

            @pl.when(travels(d, way, d + 1))
            def _():
                @pl.when(d > 0)
                def _():
                    chain(d, way, unit, 0).wait_send()

                chain(d, way, unit, 1).wait_send()

    def settle_extras(slot, s):
        @pl.when(s == 0)
        def _():
            extra(slot, 1).wait_send()

            @pl.when(has_partner)
            def _():
                extra(slot, 2).wait_send()

        @pl.when(s == 1)
        def _():
            extra(slot, 0).wait_send()

    def settle_sends(some_mine, sem):
        @pl.when(some_mine)
        def _():
            await_bytes(query.at[0, pl.ds(0, tile - rows)], sem)

        @pl.when(jnp.logical_not(some_mine))
        def _():
            await_bytes(query.at[0], sem)

    def settle_deals():
        def settle_raw(i):
            for way in range(2):

                @pl.when(travels(0, way, 1))
                def _():
                    raw(way, i).wait_send()

        loop(0, WT, settle_raw)
        for head in range(3):
            settle_sends(mine[head], query_send.at[head])
            settle_sends(mine[head], value_send.at[head])
            settle_sends(mine[head], key_send.at[0, head])
            for way in range(2):

                @pl.when(travels(1, way, 1))
                def _():
                    settle_sends(mine[head], key_send.at[1 + way, head])

    def work(plane, place, idle):
        def await_extra(which):
            @pl.when(plane == 0)
            def _():
                extra(0, which).wait_recv()

            for way in range(2):

                @pl.when(used(plane, way))
                def _():
                    extra(slot_of(plane, way), which).wait_recv()

        def one(i):
            @pl.when(i == 3)
            def _():
                await_extra(1)

                @pl.when(has_partner)
                def _():
                    await_extra(2)

            @pl.when(i == 5)
            def _():
                await_extra(0)

            @pl.when(plane == 0)
            def _():
                attend(i, plane, (0,))

            @pl.when(plane > 0)
            def _():
                attend(i, plane, (0, 1))

            @pl.when((plane == far) & ((i == 4) | (i >= 6)))
            def _():
                deliver(jnp.where(i == 4, 2, jnp.where(i == 6, outer, inner)))

        first = jnp.where(place == 0, 0, jnp.where(place == 1, 1, place + 3))
        last = jnp.where(place == 0, 1, jnp.where(place == 1, 5, 2 * place + 2))
        loop(first, jnp.where(idle, first, last), one)

    def arrive(d, s, unit):
        for way in range(2):
            on = travels(d, way, d + 1)

            @pl.when(travels(d, way, d))
            def _():
                for which in range(2):
                    chain(d - 1, way, unit, which).wait_recv()

                    @pl.when(on)
                    def _():
                        chain(d, way, unit, which).start()

            @pl.when(used(d, way))
            def _():
                start_extras(slot_of(d, way), s)

        settle_chain(d - 2, unit)

        @pl.when(d == R)
        def _():
            settle_extras(0, s)

            @pl.when(s == 0)
            def _():
                settle_deals()

        for way in range(2):

            @pl.when(used(d - 1, way))
            def _():
                settle_extras(slot_of(d - 1, way), s)

    def step(d, place):
        s = jnp.where(place == 3, 2, place)
        unit = unit_at(s)

        def phase(turn):
            @pl.when((turn == 0) & (d == 2) & (place != 2))
            def _():
                @pl.when(s == 0)
                def _():
                    await_bytes(query, query_recv)

                await_bytes(kv.at[0, unit, 0], key_recv.at[0, unit])
                start_extras(0, s)

            @pl.when((turn == 1) & (place != 2))
            def _():
                arrive(d, s, unit)

            idle = ((turn == 0) & (d > 3)) | ((turn == 1) & (d == 2))
            work(jnp.where(turn == 1, d, jnp.where(d == 2, 1, 0)), place, idle)

        loop(0, 2, phase)

    def hop(d):
        loop(0, 4, lambda place: step(d, place))

    loop(2, far + 1, hop)

    def settle_last(s):
        settle_chain(far - 1, s)
        for way in range(2):

            @pl.when(used(far, way))
            def _():
                settle_extras(slot_of(far, way), s)

    loop(0, 3, settle_last)
    loop(0, 3, lambda unit: settle_sends(column_of(unit) == x, out_send.at[unit]))
    await_bytes(out, out_recv)


def attention(rows_of_tiles, frames, parts, queries, keys, values, windows, counts):
    rows, width = queries.shape
    tile = rows * parts
    far = rows_of_tiles + 1
    slots = 1 + 2 * far
    any_space = pl.BlockSpec(memory_space=pltpu.HBM)
    dma = pltpu.SemaphoreType.DMA
    return pl.pallas_call(
        functools.partial(kernel, rows_of_tiles, frames, parts),
        out_shape=pltpu.VMEM((rows, width), jnp.bfloat16),
        in_specs=[any_space] * 5,
        out_specs=pl.BlockSpec(memory_space=pltpu.VMEM),
        scratch_shapes=[
            pltpu.VMEM((1, WINDOW), jnp.int32),
            pltpu.VMEM((1, 1), jnp.int32),
            pltpu.VMEM((slots, 6, 2, tile, HEAD_DIM), jnp.bfloat16),
            pltpu.VMEM((2, rows, width), jnp.bfloat16),
            pltpu.VMEM((3, tile, HEAD_DIM), jnp.bfloat16),
            pltpu.VMEM((3, tile, HEAD_DIM), jnp.bfloat16),
            pltpu.VMEM((WT, FLAG_ROWS, HEAD_DIM), jnp.float32),
            pltpu.VMEM((3, 1, tile), jnp.float32),
            pltpu.VMEM((3, HEAD_DIM + SUM_ROWS, tile), jnp.float32),
            pltpu.VMEM((3, tile, HEAD_DIM), jnp.bfloat16),
            dma((2,)),
            dma((WT - 1,)),
            dma((WT - 1,)),
            dma((2, WT)),
            dma((2, WT)),
            dma((3, 3)),
            dma((3, 3)),
            dma((3,)),
            dma((3,)),
            dma,
            dma((3,)),
            dma((2, far, 3, 2)),
            dma((2, far, 3, 2)),
            dma((slots, 3)),
            dma((slots, 3)),
            dma,
            dma((3,)),
        ],
        compiler_params=pltpu.CompilerParams(
            collective_id=0, has_side_effects=True, vmem_limit_bytes=60 * 1024 * 1024
        ),
    )(windows, counts.reshape(1, 1), queries, keys, values)


def solution(mesh):
    split = P(("frame", "head"), None)
    return jax.shard_map(
        functools.partial(attention, HT, mesh.shape["frame"], mesh.shape["head"]),
        mesh=mesh,
        in_specs=(split, split, split, P("frame", None), P("frame")),
        out_specs=split,
        check_vma=False,
    )
```
